32 devices in a mesh: cp: 16 (over z, y, x), tp: 2 (over core).
Axes of the slice: x: 2, y: 2, z: 4, core: 2. Of those that a mesh axis runs over, the one named last changes fastest.
Arguments:
- hidden_states: bfloat16 [2048, 4096], P('cp', 'tp'), may hold values from -18 to 18
- query: bfloat16 [2048, 4096], P('cp', 'tp'), may hold values from -300 to 300
- attention_output_gradient: bfloat16 [2048, 4096], P('cp', 'tp'), may hold values from -6 to 6
- key_weight: bfloat16 [4096, 512], P('cp', 'tp'), may hold values from -0.09375 to 0.09375
- value_projection_weight: bfloat16 [4096, 512], P('cp', 'tp'), may hold values from -0.09375 to 0.09375
- doc_start: int32 [2048], P('cp'), may hold values from 0 to 2047, as said below
Outputs:
- grad_query: bfloat16 [2048, 4096], P('cp', 'tp')
- grad_hidden: bfloat16 [2048, 4096], P('cp')
- grad_key_weight: float32 [4096, 512], P('cp', 'tp')
- grad_value_weight: float32 [4096, 512], P('cp', 'tp')
The draws below stay inside these ranges and needn't reach their ends.
Inputs may be any that keep to these rules, and one draw needn't show every extreme that they name: `doc_start`: each entry is the position of the first token of that token's document; documents are runs of consecutive tokens; no document holds tokens on both sides of a multiple of 1024; one document has exactly 1024 tokens; the last token is a document of its own.
All inputs are finite; a program needn't handle non-finite values.
Results may differ from the reference program's by a relative error of at most 0.0071.
Values may be sent and summed in bfloat16 or wider, within the bound.
A program may use at most 64 MiB of HBM per device.

```python
import jax
import jax.numpy as jnp
from jax import lax

MODEL_WIDTH = 4096
QUERY_HEAD_COUNT = 32
KEY_VALUE_HEADS = 4
HEAD_SIZE = 128
TOKENS_PER_SHARD = 128
GROUP = 8
PACKED_TOKENS = 2048
N_CP = 16


def shared_draws(key):
    states_key, weight_random_key, pair_key = jax.random.split(key, 3)
    base_states = jnp.clip(jax.random.normal(states_key, (PACKED_TOKENS, MODEL_WIDTH), jnp.float32), -6.0, 6.0)
    pairing = jax.random.permutation(pair_key, N_CP)
    token_owner = jnp.arange(PACKED_TOKENS) // TOKENS_PER_SHARD
    feature_owner = jnp.arange(MODEL_WIDTH) // (MODEL_WIDTH // N_CP)
    boosted = jnp.where(pairing[token_owner][:, None] == feature_owner[None, :], 3.0, 1.0)
    weight_matrices = jnp.clip(jax.random.normal(weight_random_key, (MODEL_WIDTH, KEY_VALUE_HEADS * HEAD_SIZE), jnp.float32), -6.0, 6.0) * MODEL_WIDTH ** (-0.5)
    return (base_states * boosted, weight_matrices)


def draw_hidden_states(key, part):
    states, unused_weights = shared_draws(key)
    return states.astype(jnp.bfloat16)


def draw_key_weight(key, part):
    unused_states, weight_matrices = shared_draws(key)
    return weight_matrices.astype(jnp.bfloat16)


def draw_query(key, part):
    key = jax.random.fold_in(key, 5)
    return jnp.clip(jax.random.normal(key, (PACKED_TOKENS, QUERY_HEAD_COUNT * HEAD_SIZE), jnp.float32), -6.0, 6.0).astype(jnp.bfloat16)


def draw_doc_start(key, part):
    key = jax.random.fold_in(key, 11)
    level_key, long_key, pick_key = jax.random.split(key, 3)
    block_len = GROUP * TOKENS_PER_SHARD
    total_block_count = PACKED_TOKENS // block_len
    positions = jnp.arange(PACKED_TOKENS, dtype=jnp.int32)
    owner = positions // block_len
    levels = jax.random.randint(level_key, (total_block_count,), 1, 4)
    period = jnp.maximum(block_len // 2 ** levels, 2).astype(jnp.int32)
    long_block = jax.random.randint(long_key, (), 0, total_block_count - 1)
    picks = jax.random.randint(pick_key, (PACKED_TOKENS,), 0, 1 << 20)
    starts_here = (picks % period[owner] == 0) & (owner != long_block)
    starts_here = starts_here | (positions % block_len == 0) | (positions == PACKED_TOKENS - 1)
    return lax.cummax(jnp.where(starts_here, positions, 0), axis=0).astype(jnp.int32)


def shard_levels(rng, extent, pieces, low, high):
    level = 1.0
    for axis_at, parts in pieces:
        draws = jax.random.uniform(jax.random.fold_in(jax.random.fold_in(rng, 6), axis_at), (parts,), jnp.float32, low / len(pieces), high / len(pieces))
        level = level * jnp.repeat(jnp.exp(draws), extent[axis_at] // parts).reshape((-1,) + (1,) * (len(extent) - 1 - axis_at))
    return level


def bell_draw(stream_key, shape, spread, reach, cuts=(), held_as=jnp.bfloat16):
    gain = shard_levels(stream_key, shape, cuts, -0.22, 0.18) if cuts else 1.0
    entries = jax.random.normal(stream_key, shape, jnp.float32) * spread * gain
    return jnp.minimum(jnp.maximum(entries, -reach), reach).astype(held_as)


def setup_inputs(seed: int = 0) -> dict:
    streams_of = jax.random.split(jax.random.key(seed), 7)
    hidden_states = draw_hidden_states(jax.random.fold_in(streams_of[6], 71), 0)
    query = draw_query(jax.random.fold_in(streams_of[6], 71), 0)
    attention_output_gradient = bell_draw(streams_of[2], (PACKED_TOKENS, QUERY_HEAD_COUNT * HEAD_SIZE), 1.0, 6.0, ((0, 16), (1, 2)))
    key_weight = draw_key_weight(jax.random.fold_in(streams_of[6], 71), 0)
    value_projection_weight = bell_draw(streams_of[4], (MODEL_WIDTH, KEY_VALUE_HEADS * HEAD_SIZE), MODEL_WIDTH ** -0.5, 0.09375, ((0, 16), (1, 2)))
    doc_start = draw_doc_start(jax.random.fold_in(streams_of[6], 71), 0)
    return {"hidden_states": hidden_states, "query": query, "attention_output_gradient": attention_output_gradient, "key_weight": key_weight, "value_projection_weight": value_projection_weight, "doc_start": doc_start}


NEG_FILL = -1e+30

def rounded(values_in):
    return lax.optimization_barrier(values_in.astype(jnp.bfloat16)).astype(jnp.float32)

def reference(hidden_states, query, attention_output_gradient, key_weight, value_projection_weight, doc_start):
    highest = lax.Precision.HIGHEST
    inv_sqrt = HEAD_SIZE ** (-0.5)
    query_per_key_heads = QUERY_HEAD_COUNT // KEY_VALUE_HEADS
    key_rows = jnp.dot(hidden_states, key_weight, preferred_element_type=jnp.float32).astype(jnp.bfloat16)
    value_rows = jnp.dot(hidden_states, value_projection_weight, preferred_element_type=jnp.float32).astype(jnp.bfloat16)
    total_block_count = PACKED_TOKENS // TOKENS_PER_SHARD
    window_length = GROUP * TOKENS_PER_SHARD
    leading_rows = (GROUP - 1) * TOKENS_PER_SHARD
    padding_rows = jnp.zeros((leading_rows, KEY_VALUE_HEADS * HEAD_SIZE), jnp.bfloat16)
    padded_key_rows = jnp.concatenate([padding_rows, key_rows], axis=0)
    padded_value_rows = jnp.concatenate([padding_rows, value_rows], axis=0)
    query_block_list = query.reshape(total_block_count, TOKENS_PER_SHARD, KEY_VALUE_HEADS, query_per_key_heads, HEAD_SIZE)
    gradient_block_list = attention_output_gradient.reshape(total_block_count, TOKENS_PER_SHARD, KEY_VALUE_HEADS, query_per_key_heads, HEAD_SIZE)
    start_blocks = doc_start.reshape(total_block_count, TOKENS_PER_SHARD)

    def one_block(sums_now, inputs):
        block_index, query_block, grad_block, start_block = inputs
        leading_row = (block_index * TOKENS_PER_SHARD).astype(jnp.int32)
        key_span_rows = lax.dynamic_slice_in_dim(padded_key_rows, leading_row, window_length, 0).astype(jnp.float32).reshape(window_length, KEY_VALUE_HEADS, HEAD_SIZE)
        value_span_rows = lax.dynamic_slice_in_dim(padded_value_rows, leading_row, window_length, 0).astype(jnp.float32).reshape(window_length, KEY_VALUE_HEADS, HEAD_SIZE)
        query_pos = leading_row + jnp.arange(TOKENS_PER_SHARD, dtype=jnp.int32)
        key_pos = leading_row - leading_rows + jnp.arange(window_length, dtype=jnp.int32)
        visible = (key_pos[None, :] >= start_block[:, None]) & (key_pos[None, :] <= query_pos[:, None])
        query_float = query_block.astype(jnp.float32)
        grad_float = grad_block.astype(jnp.float32)
        scores = jnp.einsum('qgrd,kgd->grqk', query_float, key_span_rows, precision=highest) * inv_sqrt
        scores = jnp.where(visible, scores, NEG_FILL)
        top_score = lax.optimization_barrier(jnp.max(scores, axis=-1, keepdims=True))
        log_total = top_score + jnp.log(lax.optimization_barrier(jnp.sum(jnp.where(visible, jnp.exp(scores - top_score), 0.0), axis=-1, keepdims=True)))
        probs_now = jnp.where(visible, jnp.exp(scores - log_total), 0.0)
        attended = jnp.einsum('grqk,kgd->grqd', probs_now, value_span_rows, precision=highest)
        delta_rows = jnp.einsum('qgrd,grqd->grq', grad_float, attended, precision=highest)
        probs_rounded = rounded(probs_now)
        value_gradient_total = jnp.einsum('grqk,qgrd->kgd', probs_rounded, grad_float, precision=highest)
        prob_grad = jnp.einsum('qgrd,kgd->grqk', grad_float, value_span_rows, precision=highest)
        score_grad = rounded(probs_now * (prob_grad - delta_rows[..., None]))
        query_grad = jnp.einsum('grqk,kgd->qgrd', score_grad, key_span_rows, precision=highest) * inv_sqrt
        key_gradient_total = jnp.einsum('grqk,qgrd->kgd', score_grad, query_float, precision=highest) * inv_sqrt
        paired_gradient = jnp.concatenate([key_gradient_total.reshape(window_length, KEY_VALUE_HEADS * HEAD_SIZE), value_gradient_total.reshape(window_length, KEY_VALUE_HEADS * HEAD_SIZE)], axis=1)
        current = lax.dynamic_slice_in_dim(sums_now, leading_row, window_length, 0)
        sums_now = lax.dynamic_update_slice_in_dim(sums_now, current + paired_gradient, leading_row, 0)
        return (sums_now, query_grad.reshape(TOKENS_PER_SHARD, QUERY_HEAD_COUNT * HEAD_SIZE))
    starting_carry = jnp.zeros((leading_rows + PACKED_TOKENS, 2 * KEY_VALUE_HEADS * HEAD_SIZE), jnp.float32)
    block_ids = jnp.arange(total_block_count, dtype=jnp.int32)
    sums_final, query_grads = lax.scan(one_block, starting_carry, (block_ids, query_block_list, gradient_block_list, start_blocks))
    grad_query = query_grads.reshape(PACKED_TOKENS, QUERY_HEAD_COUNT * HEAD_SIZE).astype(jnp.bfloat16)
    gradients_lowered = sums_final[leading_rows:].astype(jnp.bfloat16)
    key_gradient_lowered = gradients_lowered[:, :KEY_VALUE_HEADS * HEAD_SIZE]
    value_gradient_lowered = gradients_lowered[:, KEY_VALUE_HEADS * HEAD_SIZE:]
    grad_key_weight = jnp.dot(hidden_states.T, key_gradient_lowered, preferred_element_type=jnp.float32)
    grad_value_weight = jnp.dot(hidden_states.T, value_gradient_lowered, preferred_element_type=jnp.float32)
    grad_hidden = (jnp.dot(key_gradient_lowered, key_weight.T, preferred_element_type=jnp.float32) + jnp.dot(value_gradient_lowered, value_projection_weight.T, preferred_element_type=jnp.float32)).astype(jnp.bfloat16)
    return (grad_query, grad_hidden, grad_key_weight, grad_value_weight)
```

```python
import functools

import jax
import jax.numpy as jnp
from jax import lax
from jax.experimental import pallas as pl
from jax.experimental.pallas import tpu as pltpu
from jax.sharding import PartitionSpec as P

HEAD_SIZE = 128
SPAN = 8


NEG_FILL = -1e30


def passed_along(value, axis, steps):
    count = lax.axis_size(axis)
    leading, last = (max(0, -steps), min(count, count - steps))
    return lax.ppermute(value, axis, [(source, source + steps) for source in range(leading, last)])


def from_behind(block, axis, distance):
    devices = range(lax.axis_size(axis))
    route = [((i - distance) % len(devices), i) for i in devices]
    return lax.ppermute(block, axis, route)


def split_pair(kv_block, heads_kv):
    row_count = kv_block.shape[0]
    kv_width = kv_block.shape[1] // 2
    key_part = kv_block[:, :kv_width].reshape(row_count, heads_kv, HEAD_SIZE)
    value_part = kv_block[:, kv_width:].reshape(row_count, heads_kv, HEAD_SIZE)
    return (key_part, value_part)


def forward_tile(running, query_heads, kv_block, visible_now, inv_sqrt):
    row_max, row_total, weighted = running
    key_part, value_part = split_pair(kv_block, query_heads.shape[1])
    scores = (
        jnp.einsum("qgrd,kgd->grqk", query_heads, key_part, preferred_element_type=jnp.float32)
        * inv_sqrt
    )
    scores = jnp.where(visible_now, scores, NEG_FILL)
    new_max = jnp.maximum(row_max, jnp.max(scores, axis=-1))
    probs_now = jnp.where(visible_now, jnp.exp(scores - new_max[..., None]), 0.0)
    fading = jnp.exp(row_max - new_max)
    new_total = row_total * fading + jnp.sum(probs_now, axis=-1)
    added = jnp.einsum(
        "grqk,kgd->grqd", probs_now, value_part.astype(jnp.float32), precision=lax.Precision.HIGHEST
    )
    return (new_max, new_total, weighted * fading[..., None] + added)


def backward_tile(query_heads, grad_heads, log_total, delta_rows, kv_block, visible_now, inv_sqrt):
    row_count = query_heads.shape[0]
    key_part, value_part = split_pair(kv_block, query_heads.shape[1])
    scores = (
        jnp.einsum("qgrd,kgd->grqk", query_heads, key_part, preferred_element_type=jnp.float32)
        * inv_sqrt
    )
    scores = jnp.where(visible_now, scores, NEG_FILL)
    probs_now = jnp.where(visible_now, jnp.exp(scores - log_total[..., None]), 0.0)
    value_gradient_total = jnp.einsum(
        "grqk,qgrd->kgd",
        probs_now.astype(jnp.bfloat16),
        grad_heads,
        preferred_element_type=jnp.float32,
    )
    prob_grad = jnp.einsum(
        "qgrd,kgd->grqk", grad_heads, value_part, preferred_element_type=jnp.float32
    )
    score_grad = (probs_now * (prob_grad - delta_rows[..., None])).astype(jnp.bfloat16)
    query_grad = (
        jnp.einsum("grqk,kgd->qgrd", score_grad, key_part, preferred_element_type=jnp.float32)
        * inv_sqrt
    )
    key_gradient_total = (
        jnp.einsum("grqk,qgrd->kgd", score_grad, query_heads, preferred_element_type=jnp.float32)
        * inv_sqrt
    )
    paired_gradient = jnp.concatenate(
        [key_gradient_total.reshape(row_count, -1), value_gradient_total.reshape(row_count, -1)],
        axis=1,
    )
    return (query_grad.reshape(row_count, -1), paired_gradient)


def per_device(
    hidden_states, query, attention_output_gradient, key_weight, value_projection_weight, doc_start
):
    row_count = query.shape[0]
    node_count = lax.axis_size("cp")
    my_index = lax.axis_index("cp")
    chain_len = min(SPAN, node_count // 2)
    kv_width = key_weight.shape[1]
    heads_kv = kv_width // HEAD_SIZE
    query_per_key_heads = query.shape[1] // kv_width
    inv_sqrt = HEAD_SIZE ** (-0.5)
    features = lax.all_gather(hidden_states, "tp", axis=1, tiled=True)
    key_full, value_full = (
        lax.all_gather(key_weight, "cp", axis=0, tiled=True),
        lax.all_gather(value_projection_weight, "cp", axis=0, tiled=True),
    )
    key_rows = jnp.dot(features, key_full, preferred_element_type=jnp.float32).astype(jnp.bfloat16)
    value_rows = jnp.dot(features, value_full, preferred_element_type=jnp.float32).astype(
        jnp.bfloat16
    )
    local_block = jnp.concatenate([key_rows, value_rows], axis=1)
    query_heads = query.reshape(row_count, heads_kv, query_per_key_heads, HEAD_SIZE)
    grad_heads = attention_output_gradient.reshape(
        row_count, heads_kv, query_per_key_heads, HEAD_SIZE
    )
    offsets = jnp.arange(row_count, dtype=jnp.int32)
    query_pos = my_index * row_count + offsets

    def visible(turn_index):
        source = my_index - turn_index
        key_pos = source * row_count + offsets
        return (
            (key_pos[None, :] >= doc_start[:, None])
            & (key_pos[None, :] <= query_pos[:, None])
            & (source >= 0)
        )

    start_stats = (
        jnp.full((heads_kv, query_per_key_heads, row_count), NEG_FILL, jnp.float32),
        jnp.zeros((heads_kv, query_per_key_heads, row_count), jnp.float32),
        jnp.zeros((heads_kv, query_per_key_heads, row_count, HEAD_SIZE), jnp.float32),
    )
    running = forward_tile(start_stats, query_heads, local_block, visible(0), inv_sqrt)
    stored = jnp.zeros((1,), jnp.bfloat16)

    def forward_turn(turn_index, carried):
        kv_block, stats_now, stored_now = carried
        kv_block = passed_along(kv_block, "cp", 1)
        visible_now = visible(turn_index)
        stats_now = lax.cond(
            jnp.any(visible_now),
            lambda: forward_tile(stats_now, query_heads, kv_block, visible_now, inv_sqrt),
            lambda: stats_now,
        )
        return (kv_block, stats_now, stored_now)

    unused_block, running, stored = lax.fori_loop(
        1, chain_len, forward_turn, (local_block, running, stored)
    )
    row_max, row_total, weighted = running
    log_total = row_max + jnp.log(row_total)
    attended = weighted / row_total[..., None]
    delta_rows = jnp.einsum(
        "qgrd,grqd->grq", grad_heads.astype(jnp.float32), attended, precision=lax.Precision.HIGHEST
    )
    query_sum, kv_sums = backward_tile(
        query_heads, grad_heads, log_total, delta_rows, local_block, visible(0), inv_sqrt
    )

    def backward_turn(turn_index, carried):
        kv_block, sums_now, query_now = carried
        sums_now = from_behind(sums_now, "cp", 1)
        kv_block = passed_along(kv_block, "cp", 1)
        visible_now = visible(turn_index)
        query_part, pair_part = lax.cond(
            jnp.any(visible_now),
            lambda: backward_tile(
                query_heads, grad_heads, log_total, delta_rows, kv_block, visible_now, inv_sqrt
            ),
            lambda: (jnp.zeros_like(query_now), jnp.zeros_like(sums_now)),
        )
        return (kv_block, sums_now + pair_part, query_now + query_part)

    unused_last, kv_sums, query_sum = lax.fori_loop(
        1, chain_len, backward_turn, (local_block, kv_sums, query_sum)
    )
    returned = from_behind(kv_sums.astype(jnp.bfloat16), "cp", 1 - chain_len).astype(kv_sums.dtype)
    gradients_lowered = returned.astype(jnp.bfloat16)
    weight_sums = lax.psum_scatter(
        lax.dot_general(
            features,
            gradients_lowered,
            (((0,), (0,)), ((), ())),
            preferred_element_type=jnp.float32,
        ),
        "cp",
        scatter_dimension=0,
        tiled=True,
    )
    projection = jnp.concatenate([key_full, value_full], axis=1)
    input_part = lax.dot_general(
        gradients_lowered, projection, (((1,), (1,)), ((), ())), preferred_element_type=jnp.float32
    )
    grad_hidden = lax.psum(input_part, "tp").astype(jnp.bfloat16)
    return (
        query_sum.astype(jnp.bfloat16),
        grad_hidden,
        weight_sums[:, :kv_width],
        weight_sums[:, kv_width:],
    )


PLANE = 4


def fused_fits(mesh, model_width, tokens):
    cp, tp = mesh.shape["cp"], mesh.shape["tp"]
    if cp % SPAN or cp % (PLANE * tp) or SPAN % PLANE or tp != 2:
        return False
    return model_width % (cp * HEAD_SIZE) == 0 and tokens // cp == HEAD_SIZE


def exchange_kernel(
    count_cp,
    kv_heads,
    q_per_kv,
    hid,
    qry,
    gout,
    wk,
    wv,
    starts,
    dq_out,
    gh_out,
    gwk_out,
    gwv_out,
    xp,
    wz,
    wo,
    part,
    summed,
    kvg,
    qs,
    gs,
    s_scr,
    dp_scr,
    dqt,
    dpart,
    dsend,
    drecv,
    dkvp,
    gwown,
    gws,
    gwr,
    ghs,
    gho,
    x_send,
    x_recv,
    w_send,
    w_recv,
    o_send,
    o_recv,
    r_send,
    r_recv,
    k_send,
    k_recv,
    d_send,
    d_recv,
    p_send,
    p_recv,
    g_send,
    g_recv,
    h_send,
    h_recv,
):
    tokens = hid.shape[0]
    depth = wk.shape[0]
    half = wk.shape[1]
    cols = count_cp // PLANE
    per_tp = cols // 2
    stack = q_per_kv * tokens
    inv_sqrt = HEAD_SIZE ** (-0.5)
    f32 = jnp.float32
    bf16 = jnp.bfloat16
    c = lax.axis_index("cp")
    t = lax.axis_index("tp")
    ot = 1 - t
    z = c // PLANE
    p = c % PLANE
    j = c % SPAN
    base = c - j

    def remote(src, dst, ss, rs, cp, tp):
        return pltpu.make_async_remote_copy(
            src_ref=src,
            dst_ref=dst,
            send_sem=ss,
            recv_sem=rs,
            device_id=(cp, tp),
            device_id_type=pl.DeviceIdType.MESH,
        )

    def at_plane(pp):
        return z * PLANE + pp

    barrier = pltpu.get_barrier_semaphore()
    greeted = 0

    def greet(cp, tp):
        pl.semaphore_signal(
            barrier, inc=1, device_id=(cp, tp), device_id_type=pl.DeviceIdType.MESH
        )

    for d in range(1, SPAN):
        greet(base + (j + d) % SPAN, t)
        greeted += 1
    for d in range(PLANE):
        greet(at_plane((p + d) % PLANE), ot)
        greeted += 1
    planes = SPAN // PLANE
    for d in range(cols - planes):
        greet((((z // planes) * planes + planes + d) % cols) * PLANE + p, t)
        greeted += 1
    wz[z, :, :half] = wk[...]
    wz[z, :, half:] = wv[...]
    pl.semaphore_wait(barrier, greeted)

    sends = []

    for d in range(1, cols):
        copy = remote(
            wz.at[z],
            wz.at[z],
            w_send.at[d],
            w_recv.at[z],
            ((z + d) % cols) * PLANE + p,
            t,
        )
        copy.start()
        sends.append(copy)
    for tt in range(2):
        for d in range(PLANE):
            if tt == 0 and d == 0:
                continue
            pp = (p + d) % PLANE
            for k in range(per_tp):
                lane = pl.multiple_of((k * PLANE + pp) * depth, HEAD_SIZE)
                copy = remote(
                    hid.at[:, pl.ds(lane, depth)],
                    xp.at[t * per_tp + k, p],
                    x_send.at[tt, d, k],
                    x_recv.at[t, p, k],
                    at_plane(pp),
                    (t + tt) % 2,
                )
                copy.start()
                sends.append(copy)
    for k in range(per_tp):
        lane = pl.multiple_of((k * PLANE + p) * depth, HEAD_SIZE)
        xp[t * per_tp + k, p] = hid[:, pl.ds(lane, depth)]
    for h in range(kv_heads * q_per_kv):
        g, r = h // q_per_kv, h % q_per_kv
        lanes = slice(h * HEAD_SIZE, (h + 1) * HEAD_SIZE)
        qs[g, r * tokens : (r + 1) * tokens] = qry[:, lanes]
        gs[g, r * tokens : (r + 1) * tokens] = gout[:, lanes]

    for tt in range(2):
        for d in range(PLANE):
            if tt == 0 and d == 0:
                continue
            src_t, src_p = (t + tt) % 2, (p + d) % PLANE
            for k in range(per_tp):
                slot = xp.at[src_t * per_tp + k, src_p]
                remote(
                    slot, slot, x_send.at[tt, d, k], x_recv.at[src_t, src_p, k], at_plane(src_p), src_t if tt else t
                ).wait_recv()

    def project(zz, first):
        lhs = xp[zz].reshape(PLANE * tokens, depth)
        add = jnp.dot(lhs, wz[zz], preferred_element_type=f32).reshape(part.shape)
        if first:
            part[...] = add
        else:
            part[...] += add

    project(z, True)
    for d in range(1, cols):
        zz = (z + d) % cols
        remote(wz.at[zz], wz.at[zz], w_send.at[d], w_recv.at[zz], zz * PLANE + p, t).wait_recv()
        project(zz, False)
    for d in range(1, PLANE):
        pp = (p + d) % PLANE
        copy = remote(part.at[pp], summed.at[p], r_send.at[d], r_recv.at[p], at_plane(pp), t)
        copy.start()
        sends.append(copy)
    for k in range(per_tp):
        copy = remote(wz.at[ot * per_tp + k], wo.at[k], o_send.at[k], o_recv.at[k], c, ot)
        copy.start()
        sends.append(copy)
    total = part[p]
    for d in range(1, PLANE):
        pp = (p + d) % PLANE
        remote(
            summed.at[pp], summed.at[pp], r_send.at[d], r_recv.at[pp], at_plane(pp), t
        ).wait_recv()
        total = total + summed[pp]
    kvg[j] = total.astype(bf16)

    def kv_copy(d):
        return remote(kvg.at[j], kvg.at[j], k_send.at[d], k_recv.at[j], c + d, t)

    for d in range(1, SPAN):

        @pl.when(j + d < SPAN)
        def _():
            kv_copy(d).start()

    for d in range(1, SPAN):

        @pl.when(j >= d)
        def _():
            slot = kvg.at[j - d]
            remote(slot, slot, k_send.at[d], k_recv.at[j - d], c - d, t).wait_recv()

    row = lax.broadcasted_iota(jnp.int32, (tokens, tokens), 0)
    lane = lax.broadcasted_iota(jnp.int32, (tokens, tokens), 1)
    start_row = starts[...]

    def fold(value, op):
        return op(value.reshape(tokens // 8, 8, stack), axis=0)

    nt = (((1,), (1,)), ((), ()))
    tn = (((0,), (0,)), ((), ()))
    for g in range(kv_heads):
        kcol = slice(g * HEAD_SIZE, (g + 1) * HEAD_SIZE)
        vcol = slice(half + g * HEAD_SIZE, half + (g + 1) * HEAD_SIZE)

        def first_pass(i, top):
            key_pos = (base + i) * tokens + row
            seen = (key_pos >= start_row) & (key_pos <= c * tokens + lane)
            bias = jnp.where(seen, 0.0, NEG_FILL)
            bias = jnp.concatenate([bias] * q_per_kv, axis=1)
            s = lax.dot_general(kvg[i, :, kcol], qs[g], nt, preferred_element_type=f32)
            s = s * inv_sqrt + bias
            s_scr[i] = s
            dp_scr[i] = lax.dot_general(kvg[i, :, vcol], gs[g], nt, preferred_element_type=f32)
            return jnp.maximum(top, fold(s, jnp.max))

        top = lax.fori_loop(0, j + 1, first_pass, jnp.full((8, stack), NEG_FILL, f32))
        top = jnp.max(top, axis=0, keepdims=True)

        def second_pass(i, carried):
            count, dot = carried
            e = jnp.exp(s_scr[i] - top)
            s_scr[i] = e
            return count + fold(e, jnp.sum), dot + fold(e * dp_scr[i], jnp.sum)

        zero = jnp.zeros((8, stack), f32)
        count, dot = lax.fori_loop(0, j + 1, second_pass, (zero, zero))
        inv_count = 1.0 / jnp.sum(count, axis=0, keepdims=True)
        delta = jnp.sum(dot, axis=0, keepdims=True) * inv_count
        dqt[...] = jnp.zeros_like(dqt)

        def third_pass(i, carried):
            probs = s_scr[i] * inv_count
            ds = (probs * (dp_scr[i] - delta)).astype(bf16)
            dpart[i, :, vcol] = jnp.dot(probs.astype(bf16), gs[g], preferred_element_type=f32)
            dpart[i, :, kcol] = jnp.dot(ds, qs[g], preferred_element_type=f32) * inv_sqrt
            dqt[...] += lax.dot_general(kvg[i, :, kcol], ds, tn, preferred_element_type=f32)
            return carried

        lax.fori_loop(0, j + 1, third_pass, 0)
        for r in range(q_per_kv):
            h = g * q_per_kv + r
            tile = dqt[:, r * tokens : (r + 1) * tokens]
            dq_out[:, h * HEAD_SIZE : (h + 1) * HEAD_SIZE] = (tile.T * inv_sqrt).astype(bf16)

    def grad_copy(d):
        return remote(dsend.at[d], drecv.at[d], d_send.at[d], d_recv.at[d], c - d, t)

    for d in range(1, SPAN):

        @pl.when(j >= d)
        def _():
            dsend[d] = dpart[j - d].astype(bf16)
            grad_copy(d).start()

    dpart[0] = dpart[j]
    for d in range(1, SPAN):

        @pl.when(j + d < SPAN)
        def _():
            slot = drecv.at[d]
            remote(slot, slot, d_send.at[d], d_recv.at[d], c + d, t).wait_recv()
            dpart[0] += drecv[d].astype(f32)

    dkvp[t, p] = dpart[0].astype(bf16)
    for tt in range(2):
        for d in range(PLANE):
            if tt == 0 and d == 0:
                continue
            copy = remote(
                dkvp.at[t, p],
                dkvp.at[t, p],
                p_send.at[tt, d],
                p_recv.at[t, p],
                at_plane((p + d) % PLANE),
                (t + tt) % 2,
            )
            copy.start()
            sends.append(copy)

    def wait_plane(tt):
        for d in range(1 - tt, PLANE):
            src_t, src_p = (t + tt) % 2, (p + d) % PLANE
            slot = dkvp.at[src_t, src_p]
            remote(
                slot, slot, p_send.at[tt, d], p_recv.at[src_t, src_p], at_plane(src_p), src_t
            ).wait_recv()

    wait_plane(0)
    mine = dkvp[t].reshape(PLANE * tokens, 2 * half)

    def weight_part(zz):
        lhs = xp[zz].reshape(PLANE * tokens, depth)
        return lax.dot_general(lhs, mine, tn, preferred_element_type=f32)

    for d in range(1, cols):
        gws[d] = weight_part((z + d) % cols).astype(bf16)
        copy = remote(
            gws.at[d],
            gwr.at[d],
            g_send.at[d],
            g_recv.at[d],
            ((z + d) % cols) * PLANE + p,
            t,
        )
        copy.start()
        sends.append(copy)
    wait_plane(1)
    for k in range(per_tp):
        remote(wo.at[k], wo.at[k], o_send.at[k], o_recv.at[k], c, ot).wait_recv()
    other = dkvp[ot].reshape(PLANE * tokens, 2 * half)
    for k in range(per_tp):
        value = lax.dot_general(mine, wz[t * per_tp + k], nt, preferred_element_type=f32)
        value = value + lax.dot_general(other, wo[k], nt, preferred_element_type=f32)
        ghs[:, k] = value.astype(bf16).reshape(PLANE, tokens, depth)
    for tt in range(2):
        for d in range(PLANE):
            if tt == 0 and d == 0:
                continue
            pp = (p + d) % PLANE
            copy = remote(
                ghs.at[pp],
                gho.at[p, t],
                h_send.at[tt, d],
                h_recv.at[p, t],
                at_plane(pp),
                (t + tt) % 2,
            )
            copy.start()
            sends.append(copy)
    gho[p, t] = ghs[p]
    gwown[...] = weight_part(z)
    for tt in range(2):
        for d in range(PLANE):
            if tt == 0 and d == 0:
                continue
            src_t, src_p = (t + tt) % 2, (p + d) % PLANE
            slot = gho.at[src_p, src_t]
            remote(
                slot, slot, h_send.at[tt, d], h_recv.at[src_p, src_t], at_plane(src_p), src_t
            ).wait_recv()
    for zz in range(cols):
        for pp in range(PLANE):
            block = (zz * PLANE + pp) * depth
            gh_out[:, block : block + depth] = gho[pp, zz // per_tp, zz % per_tp]
    total = gwown[...]
    for d in range(1, cols):
        slot = gwr.at[d]
        remote(slot, slot, g_send.at[d], g_recv.at[d], ((z + d) % cols) * PLANE + p, t).wait_recv()
        total = total + gwr[d].astype(f32)
    gwk_out[...] = total[:, :half]
    gwv_out[...] = total[:, half:]
    for copy in sends:
        copy.wait_send()
    for d in range(1, SPAN):

        @pl.when(j + d < SPAN)
        def _():
            kv_copy(d).wait_send()

        @pl.when(j >= d)
        def _():
            grad_copy(d).wait_send()


def fused_device(hidden_states, query, attention_output_gradient, key_weight, value_weight, doc_start):
    tokens, width = hidden_states.shape
    depth, half = key_weight.shape
    count_cp = lax.axis_size("cp")
    cols = count_cp // PLANE
    per_tp = cols // 2
    kv_heads = half // HEAD_SIZE
    q_per_kv = query.shape[1] // half
    stack = q_per_kv * tokens
    pair = 2 * half
    bf16, f32 = jnp.bfloat16, jnp.float32
    starts = jnp.broadcast_to(doc_start[None, :], (8, tokens))[:1]
    dma = pltpu.SemaphoreType.DMA
    vmem = pltpu.VMEM
    spec = pl.BlockSpec(memory_space=pltpu.VMEM)
    return pl.pallas_call(
        functools.partial(exchange_kernel, count_cp, kv_heads, q_per_kv),
        out_shape=(
            jax.ShapeDtypeStruct(query.shape, bf16),
            jax.ShapeDtypeStruct((tokens, 2 * width), bf16),
            jax.ShapeDtypeStruct((depth, half), f32),
            jax.ShapeDtypeStruct((depth, half), f32),
        ),
        in_specs=[spec] * 6,
        out_specs=(spec,) * 4,
        scratch_shapes=[
            vmem((cols, PLANE, tokens, depth), bf16),
            vmem((cols, depth, pair), bf16),
            vmem((per_tp, depth, pair), bf16),
            vmem((PLANE, tokens, pair), f32),
            vmem((PLANE, tokens, pair), f32),
            vmem((SPAN, tokens, pair), bf16),
            vmem((kv_heads, stack, HEAD_SIZE), bf16),
            vmem((kv_heads, stack, HEAD_SIZE), bf16),
            vmem((SPAN, tokens, stack), f32),
            vmem((SPAN, tokens, stack), f32),
            vmem((HEAD_SIZE, stack), f32),
            vmem((SPAN, tokens, pair), f32),
            vmem((SPAN, tokens, pair), bf16),
            vmem((SPAN, tokens, pair), bf16),
            vmem((2, PLANE, tokens, pair), bf16),
            vmem((depth, pair), f32),
            vmem((cols, depth, pair), bf16),
            vmem((cols, depth, pair), bf16),
            vmem((PLANE, per_tp, tokens, depth), bf16),
            vmem((PLANE, 2, per_tp, tokens, depth), bf16),
            dma((2, PLANE, per_tp)),
            dma((2, PLANE, per_tp)),
            dma((cols,)),
            dma((cols,)),
            dma((per_tp,)),
            dma((per_tp,)),
            dma((PLANE,)),
            dma((PLANE,)),
            dma((SPAN,)),
            dma((SPAN,)),
            dma((SPAN,)),
            dma((SPAN,)),
            dma((2, PLANE)),
            dma((2, PLANE)),
            dma((cols,)),
            dma((cols,)),
            dma((2, PLANE)),
            dma((PLANE, 2)),
        ],
        compiler_params=pltpu.CompilerParams(
            collective_id=0, has_side_effects=True, vmem_limit_bytes=56 * 1024 * 1024
        ),
    )(hidden_states, query, attention_output_gradient, key_weight, value_weight, starts)


def solution(mesh):
    def run(*arrays):
        fits = fused_fits(mesh, arrays[0].shape[1], arrays[0].shape[0])
        return jax.shard_map(
            fused_device if fits else per_device,
            mesh=mesh,
            in_specs=(P("cp", "tp"),) * 5 + (P("cp"),),
            out_specs=(P("cp", "tp"), P("cp", None), P("cp", "tp"), P("cp", "tp")),
            check_vma=False,
        )(*arrays)

    return run
```

```python
import functools

import jax
import jax.numpy as jnp
from jax import lax
from jax.experimental import pallas as pl
from jax.experimental.pallas import tpu as pltpu
from jax.sharding import PartitionSpec as P

HEAD_SIZE = 128
SPAN = 8


NEG_FILL = -1e30


def passed_along(value, axis, steps):
    count = lax.axis_size(axis)
    leading, last = (max(0, -steps), min(count, count - steps))
    return lax.ppermute(value, axis, [(source, source + steps) for source in range(leading, last)])


def from_behind(block, axis, distance):
    devices = range(lax.axis_size(axis))
    route = [((i - distance) % len(devices), i) for i in devices]
    return lax.ppermute(block, axis, route)


def split_pair(kv_block, heads_kv):
    row_count = kv_block.shape[0]
    kv_width = kv_block.shape[1] // 2
    key_part = kv_block[:, :kv_width].reshape(row_count, heads_kv, HEAD_SIZE)
    value_part = kv_block[:, kv_width:].reshape(row_count, heads_kv, HEAD_SIZE)
    return (key_part, value_part)


def forward_tile(running, query_heads, kv_block, visible_now, inv_sqrt):
    row_max, row_total, weighted = running
    key_part, value_part = split_pair(kv_block, query_heads.shape[1])
    scores = (
        jnp.einsum("qgrd,kgd->grqk", query_heads, key_part, preferred_element_type=jnp.float32)
        * inv_sqrt
    )
    scores = jnp.where(visible_now, scores, NEG_FILL)
    new_max = jnp.maximum(row_max, jnp.max(scores, axis=-1))
    probs_now = jnp.where(visible_now, jnp.exp(scores - new_max[..., None]), 0.0)
    fading = jnp.exp(row_max - new_max)
    new_total = row_total * fading + jnp.sum(probs_now, axis=-1)
    added = jnp.einsum(
        "grqk,kgd->grqd", probs_now, value_part.astype(jnp.float32), precision=lax.Precision.HIGHEST
    )
    return (new_max, new_total, weighted * fading[..., None] + added)


def backward_tile(query_heads, grad_heads, log_total, delta_rows, kv_block, visible_now, inv_sqrt):
    row_count = query_heads.shape[0]
    key_part, value_part = split_pair(kv_block, query_heads.shape[1])
    scores = (
        jnp.einsum("qgrd,kgd->grqk", query_heads, key_part, preferred_element_type=jnp.float32)
        * inv_sqrt
    )
    scores = jnp.where(visible_now, scores, NEG_FILL)
    probs_now = jnp.where(visible_now, jnp.exp(scores - log_total[..., None]), 0.0)
    value_gradient_total = jnp.einsum(
        "grqk,qgrd->kgd",
        probs_now.astype(jnp.bfloat16),
        grad_heads,
        preferred_element_type=jnp.float32,
    )
    prob_grad = jnp.einsum(
        "qgrd,kgd->grqk", grad_heads, value_part, preferred_element_type=jnp.float32
    )
    score_grad = (probs_now * (prob_grad - delta_rows[..., None])).astype(jnp.bfloat16)
    query_grad = (
        jnp.einsum("grqk,kgd->qgrd", score_grad, key_part, preferred_element_type=jnp.float32)
        * inv_sqrt
    )
    key_gradient_total = (
        jnp.einsum("grqk,qgrd->kgd", score_grad, query_heads, preferred_element_type=jnp.float32)
        * inv_sqrt
    )
    paired_gradient = jnp.concatenate(
        [key_gradient_total.reshape(row_count, -1), value_gradient_total.reshape(row_count, -1)],
        axis=1,
    )
    return (query_grad.reshape(row_count, -1), paired_gradient)


def per_device(
    hidden_states, query, attention_output_gradient, key_weight, value_projection_weight, doc_start
):
    row_count = query.shape[0]
    node_count = lax.axis_size("cp")
    my_index = lax.axis_index("cp")
    chain_len = min(SPAN, node_count // 2)
    kv_width = key_weight.shape[1]
    heads_kv = kv_width // HEAD_SIZE
    query_per_key_heads = query.shape[1] // kv_width
    inv_sqrt = HEAD_SIZE ** (-0.5)
    features = lax.all_gather(hidden_states, "tp", axis=1, tiled=True)
    key_full, value_full = (
        lax.all_gather(key_weight, "cp", axis=0, tiled=True),
        lax.all_gather(value_projection_weight, "cp", axis=0, tiled=True),
    )
    key_rows = jnp.dot(features, key_full, preferred_element_type=jnp.float32).astype(jnp.bfloat16)
    value_rows = jnp.dot(features, value_full, preferred_element_type=jnp.float32).astype(
        jnp.bfloat16
    )
    local_block = jnp.concatenate([key_rows, value_rows], axis=1)
    query_heads = query.reshape(row_count, heads_kv, query_per_key_heads, HEAD_SIZE)
    grad_heads = attention_output_gradient.reshape(
        row_count, heads_kv, query_per_key_heads, HEAD_SIZE
    )
    offsets = jnp.arange(row_count, dtype=jnp.int32)
    query_pos = my_index * row_count + offsets

    def visible(turn_index):
        source = my_index - turn_index
        key_pos = source * row_count + offsets
        return (
            (key_pos[None, :] >= doc_start[:, None])
            & (key_pos[None, :] <= query_pos[:, None])
            & (source >= 0)
        )

    start_stats = (
        jnp.full((heads_kv, query_per_key_heads, row_count), NEG_FILL, jnp.float32),
        jnp.zeros((heads_kv, query_per_key_heads, row_count), jnp.float32),
        jnp.zeros((heads_kv, query_per_key_heads, row_count, HEAD_SIZE), jnp.float32),
    )
    running = forward_tile(start_stats, query_heads, local_block, visible(0), inv_sqrt)
    stored = jnp.zeros((1,), jnp.bfloat16)

    def forward_turn(turn_index, carried):
        kv_block, stats_now, stored_now = carried
        kv_block = passed_along(kv_block, "cp", 1)
        visible_now = visible(turn_index)
        stats_now = lax.cond(
            jnp.any(visible_now),
            lambda: forward_tile(stats_now, query_heads, kv_block, visible_now, inv_sqrt),
            lambda: stats_now,
        )
        return (kv_block, stats_now, stored_now)

    unused_block, running, stored = lax.fori_loop(
        1, chain_len, forward_turn, (local_block, running, stored)
    )
    row_max, row_total, weighted = running
    log_total = row_max + jnp.log(row_total)
    attended = weighted / row_total[..., None]
    delta_rows = jnp.einsum(
        "qgrd,grqd->grq", grad_heads.astype(jnp.float32), attended, precision=lax.Precision.HIGHEST
    )
    query_sum, kv_sums = backward_tile(
        query_heads, grad_heads, log_total, delta_rows, local_block, visible(0), inv_sqrt
    )

    def backward_turn(turn_index, carried):
        kv_block, sums_now, query_now = carried
        sums_now = from_behind(sums_now, "cp", 1)
        kv_block = passed_along(kv_block, "cp", 1)
        visible_now = visible(turn_index)
        query_part, pair_part = lax.cond(
            jnp.any(visible_now),
            lambda: backward_tile(
                query_heads, grad_heads, log_total, delta_rows, kv_block, visible_now, inv_sqrt
            ),
            lambda: (jnp.zeros_like(query_now), jnp.zeros_like(sums_now)),
        )
        return (kv_block, sums_now + pair_part, query_now + query_part)

    unused_last, kv_sums, query_sum = lax.fori_loop(
        1, chain_len, backward_turn, (local_block, kv_sums, query_sum)
    )
    returned = from_behind(kv_sums.astype(jnp.bfloat16), "cp", 1 - chain_len).astype(kv_sums.dtype)
    gradients_lowered = returned.astype(jnp.bfloat16)
    weight_sums = lax.psum_scatter(
        lax.dot_general(
            features,
            gradients_lowered,
            (((0,), (0,)), ((), ())),
            preferred_element_type=jnp.float32,
        ),
        "cp",
        scatter_dimension=0,
        tiled=True,
    )
    projection = jnp.concatenate([key_full, value_full], axis=1)
    input_part = lax.dot_general(
        gradients_lowered, projection, (((1,), (1,)), ((), ())), preferred_element_type=jnp.float32
    )
    grad_hidden = lax.psum(input_part, "tp").astype(jnp.bfloat16)
    return (
        query_sum.astype(jnp.bfloat16),
        grad_hidden,
        weight_sums[:, :kv_width],
        weight_sums[:, kv_width:],
    )


PLANE = 4


def fused_fits(mesh, model_width, tokens):
    cp, tp = mesh.shape["cp"], mesh.shape["tp"]
    if cp % SPAN or cp % (PLANE * tp) or SPAN % PLANE or tp != 2:
        return False
    return model_width % (cp * HEAD_SIZE) == 0 and tokens // cp == HEAD_SIZE


def exchange_kernel(
    count_cp,
    kv_heads,
    q_per_kv,
    hid,
    qry,
    gout,
    wk,
    wv,
    starts,
    dq_out,
    gh_out,
    gwk_out,
    gwv_out,
    xp,
    wz,
    wo,
    part,
    summed,
    kvg,
    qs,
    gs,
    s_scr,
    dp_scr,
    dqt,
    dpart,
    dsend,
    drecv,
    dkvp,
    gwown,
    gws,
    gwr,
    ghs,
    gho,
    x_send,
    x_recv,
    w_send,
    w_recv,
    o_send,
    o_recv,
    r_send,
    r_recv,
    k_send,
    k_recv,
    d_send,
    d_recv,
    p_send,
    p_recv,
    g_send,
    g_recv,
    h_send,
    h_recv,
):
    tokens = hid.shape[0]
    depth = wk.shape[0]
    pair = 2 * HEAD_SIZE
    cols = count_cp // PLANE
    per_tp = cols // 2
    stack = q_per_kv * tokens
    inv_sqrt = HEAD_SIZE ** (-0.5)
    f32 = jnp.float32
    bf16 = jnp.bfloat16
    c = lax.axis_index("cp")
    t = lax.axis_index("tp")
    ot = 1 - t
    z = c // PLANE
    p = c % PLANE
    j = c % SPAN
    base = c - j

    def remote(src, dst, ss, rs, cp, tp):
        return pltpu.make_async_remote_copy(
            src_ref=src,
            dst_ref=dst,
            send_sem=ss,
            recv_sem=rs,
            device_id=(cp, tp),
            device_id_type=pl.DeviceIdType.MESH,
        )

    def at_plane(pp):
        return z * PLANE + pp

    barrier = pltpu.get_barrier_semaphore()
    greeted = 0

    def greet(cp, tp):
        pl.semaphore_signal(
            barrier, inc=1, device_id=(cp, tp), device_id_type=pl.DeviceIdType.MESH
        )

    for d in range(1, SPAN):
        greet(base + (j + d) % SPAN, t)
        greeted += 1
    for d in range(PLANE):
        greet(at_plane((p + d) % PLANE), ot)
        greeted += 1
    planes = SPAN // PLANE
    for d in range(cols - planes):
        greet((((z // planes) * planes + planes + d) % cols) * PLANE + p, t)
        greeted += 1
    for g in range(kv_heads):
        lanes = slice(g * HEAD_SIZE, (g + 1) * HEAD_SIZE)
        wz[g, z, :, :HEAD_SIZE] = wk[:, lanes]
        wz[g, z, :, HEAD_SIZE:] = wv[:, lanes]
    pl.semaphore_wait(barrier, greeted)

    sends = []

    def column(d):
        return ((z + d) % cols) * PLANE + p

    def plane_peers():
        return [(tt, d) for tt in range(2) for d in range(PLANE) if tt or d]

    def send_weights(g):
        for d in range(1, cols):
            slot = wz.at[g, z]
            copy = remote(slot, slot, w_send.at[g, d], w_recv.at[g, z], column(d), t)
            copy.start()
            sends.append(copy)

    send_weights(0)
    for tt, d in plane_peers():
        pp = (p + d) % PLANE
        for k in range(per_tp):
            lane = pl.multiple_of((k * PLANE + pp) * depth, HEAD_SIZE)
            copy = remote(
                hid.at[:, pl.ds(lane, depth)],
                xp.at[t * per_tp + k, p],
                x_send.at[tt, d, k],
                x_recv.at[t, p, k],
                at_plane(pp),
                (t + tt) % 2,
            )
            copy.start()
            sends.append(copy)
    for g in range(1, kv_heads):
        send_weights(g)
    for k in range(per_tp):
        lane = pl.multiple_of((k * PLANE + p) * depth, HEAD_SIZE)
        xp[t * per_tp + k, p] = hid[:, pl.ds(lane, depth)]
    for h in range(kv_heads * q_per_kv):
        g, r = h // q_per_kv, h % q_per_kv
        lanes = slice(h * HEAD_SIZE, (h + 1) * HEAD_SIZE)
        qs[g, r * tokens : (r + 1) * tokens] = qry[:, lanes]
        gs[g, r * tokens : (r + 1) * tokens] = gout[:, lanes]

    for tt, d in plane_peers():
        src_t, src_p = (t + tt) % 2, (p + d) % PLANE
        for k in range(per_tp):
            slot = xp.at[src_t * per_tp + k, src_p]
            remote(
                slot, slot, x_send.at[tt, d, k], x_recv.at[src_t, src_p, k], at_plane(src_p), src_t
            ).wait_recv()

    def project(g):
        for d in range(cols):
            zz = (z + d) % cols
            slot = wz.at[g, zz]
            if d:
                remote(slot, slot, w_send.at[g, d], w_recv.at[g, zz], column(d), t).wait_recv()
            lhs = xp[zz].reshape(PLANE * tokens, depth)
            add = jnp.dot(lhs, wz[g, zz], preferred_element_type=f32)
            add = add.reshape(PLANE, tokens, pair)
            if d:
                part[g] += add
            else:
                part[g] = add
        for d in range(1, PLANE):
            pp = (p + d) % PLANE
            copy = remote(
                part.at[g, pp], summed.at[g, p], r_send.at[g, d], r_recv.at[g, p], at_plane(pp), t
            )
            copy.start()
            sends.append(copy)
        for k in range(per_tp):
            copy = remote(
                wz.at[g, ot * per_tp + k], wo.at[g, k], o_send.at[g, k], o_recv.at[g, k], c, ot
            )
            copy.start()
            sends.append(copy)

    def kv_copy(g, d):
        slot = kvg.at[g, j]
        return remote(slot, slot, k_send.at[g, d], k_recv.at[g, j], c + d, t)

    def finish_keys(g):
        total = part[g, p]
        for d in range(1, PLANE):
            pp = (p + d) % PLANE
            slot = summed.at[g, pp]
            remote(slot, slot, r_send.at[g, d], r_recv.at[g, pp], at_plane(pp), t).wait_recv()
            total = total + summed[g, pp]
        kvg[g, j] = total.astype(bf16)
        for d in range(1, SPAN):

            @pl.when(j + d < SPAN)
            def _():
                kv_copy(g, d).start()

    row = lax.broadcasted_iota(jnp.int32, (tokens, tokens), 0)
    lane_index = lax.broadcasted_iota(jnp.int32, (tokens, tokens), 1)
    start_row = starts[...]

    def fold(value, op):
        return op(value.reshape(tokens // 8, 8, stack), axis=0)

    nt = (((1,), (1,)), ((), ()))
    tn = (((0,), (0,)), ((), ()))
    kcol = slice(0, HEAD_SIZE)
    vcol = slice(HEAD_SIZE, 2 * HEAD_SIZE)

    def grad_copy(g, d):
        return remote(
            dsend.at[g, d], drecv.at[g, d], d_send.at[g, d], d_recv.at[g, d], c - d, t
        )

    def attend(g, after_first, after_second):
        def first_pass(d, top):
            i = j - d

            @pl.when(d > 0)
            def _():
                slot = kvg.at[g, i]
                remote(slot, slot, k_send.at[g, 1], k_recv.at[g, i], c - d, t).wait_recv()

            key_pos = (base + i) * tokens + row
            seen = (key_pos >= start_row) & (key_pos <= c * tokens + lane_index)
            bias = jnp.where(seen, 0.0, NEG_FILL)
            bias = jnp.concatenate([bias] * q_per_kv, axis=1)
            s = lax.dot_general(kvg[g, i, :, kcol], qs[g], nt, preferred_element_type=f32)
            s = s * inv_sqrt + bias
            s_scr[i] = s
            dp_scr[i] = lax.dot_general(
                kvg[g, i, :, vcol], gs[g], nt, preferred_element_type=f32
            )
            return jnp.maximum(top, fold(s, jnp.max))

        top = lax.fori_loop(0, j + 1, first_pass, jnp.full((8, stack), NEG_FILL, f32))
        top = jnp.max(top, axis=0, keepdims=True)
        after_first()

        def second_pass(i, carried):
            count, dot = carried
            e = jnp.exp(s_scr[i] - top)
            s_scr[i] = e
            return count + fold(e, jnp.sum), dot + fold(e * dp_scr[i], jnp.sum)

        zero = jnp.zeros((8, stack), f32)
        count, dot = lax.fori_loop(0, j + 1, second_pass, (zero, zero))
        inv_count = 1.0 / jnp.sum(count, axis=0, keepdims=True)
        delta = jnp.sum(dot, axis=0, keepdims=True) * inv_count
        after_second()
        dqt[...] = jnp.zeros_like(dqt)

        def third_pass(i, carried):
            probs = s_scr[i] * inv_count
            ds = (probs * (dp_scr[i] - delta)).astype(bf16)
            dpart[g, i, :, vcol] = jnp.dot(probs.astype(bf16), gs[g], preferred_element_type=f32)
            dpart[g, i, :, kcol] = jnp.dot(ds, qs[g], preferred_element_type=f32) * inv_sqrt
            dqt[...] += lax.dot_general(kvg[g, i, :, kcol], ds, tn, preferred_element_type=f32)
            return carried

        lax.fori_loop(0, j + 1, third_pass, 0)
        for d in range(1, SPAN):

            @pl.when(j >= d)
            def _():
                dsend[g, d] = dpart[g, j - d].astype(bf16)
                grad_copy(g, d).start()

        for r in range(q_per_kv):
            h = g * q_per_kv + r
            tile = dqt[:, r * tokens : (r + 1) * tokens]
            dq_out[:, h * HEAD_SIZE : (h + 1) * HEAD_SIZE] = (tile.T * inv_sqrt).astype(bf16)

    def collect(g):
        dpart[g, 0] = dpart[g, j]
        for d in range(1, SPAN):

            @pl.when(j + d < SPAN)
            def _():
                slot = drecv.at[g, d]
                remote(slot, slot, d_send.at[g, d], d_recv.at[g, d], c + d, t).wait_recv()
                dpart[g, 0] += drecv[g, d].astype(f32)

        dkvp[t, g, p] = dpart[g, 0].astype(bf16)
        for tt, d in plane_peers():
            slot = dkvp.at[t, g, p]
            copy = remote(
                slot,
                slot,
                p_send.at[g, tt, d],
                p_recv.at[t, g, p],
                at_plane((p + d) % PLANE),
                (t + tt) % 2,
            )
            copy.start()
            sends.append(copy)

    def wait_plane(g, tt):
        for d in range(1 - tt, PLANE):
            src_t, src_p = (t + tt) % 2, (p + d) % PLANE
            slot = dkvp.at[src_t, g, src_p]
            remote(
                slot, slot, p_send.at[g, tt, d], p_recv.at[src_t, g, src_p], at_plane(src_p), src_t
            ).wait_recv()

    def plane_grads(tt, g):
        return dkvp[tt, g].reshape(PLANE * tokens, pair)

    def weight_part(g, zz):
        lhs = xp[zz].reshape(PLANE * tokens, depth)
        return lax.dot_general(lhs, plane_grads(t, g), tn, preferred_element_type=f32)

    def send_weight_grads(g):
        for d in range(1, cols):
            gws[g, d] = weight_part(g, (z + d) % cols).astype(bf16)
            copy = remote(
                gws.at[g, d], gwr.at[g, d], g_send.at[g, d], g_recv.at[g, d], column(d), t
            )
            copy.start()
            sends.append(copy)

    def nothing():
        pass

    last = kv_heads - 1
    project(0)
    finish_keys(0)
    for g in range(kv_heads):
        if g < last:
            project(g + 1)
        attend(
            g,
            functools.partial(finish_keys, g + 1) if g < last else nothing,
            functools.partial(collect, g - 1) if g else nothing,
        )
        if g:
            wait_plane(g - 1, 0)
            send_weight_grads(g - 1)
    collect(last)
    wait_plane(last, 0)
    send_weight_grads(last)
    for g in range(kv_heads):
        wait_plane(g, 1)
        for k in range(per_tp):
            slot = wo.at[g, k]
            remote(slot, slot, o_send.at[g, k], o_recv.at[g, k], c, ot).wait_recv()
    for k in range(per_tp):
        value = jnp.zeros((PLANE * tokens, depth), f32)
        for g in range(kv_heads):
            value += lax.dot_general(
                plane_grads(t, g), wz[g, t * per_tp + k], nt, preferred_element_type=f32
            )
            value += lax.dot_general(
                plane_grads(ot, g), wo[g, k], nt, preferred_element_type=f32
            )
        ghs[:, k] = value.astype(bf16).reshape(PLANE, tokens, depth)
    for tt, d in plane_peers():
        pp = (p + d) % PLANE
        copy = remote(
            ghs.at[pp], gho.at[p, t], h_send.at[tt, d], h_recv.at[p, t], at_plane(pp), (t + tt) % 2
        )
        copy.start()
        sends.append(copy)
    gho[p, t] = ghs[p]
    for g in range(kv_heads):
        gwown[g] = weight_part(g, z)
    for tt, d in plane_peers():
        src_t, src_p = (t + tt) % 2, (p + d) % PLANE
        slot = gho.at[src_p, src_t]
        remote(
            slot, slot, h_send.at[tt, d], h_recv.at[src_p, src_t], at_plane(src_p), src_t
        ).wait_recv()
    for zz in range(cols):
        for pp in range(PLANE):
            block = (zz * PLANE + pp) * depth
            gh_out[:, block : block + depth] = gho[pp, zz // per_tp, zz % per_tp]
    for g in range(kv_heads):
        total = gwown[g]
        for d in range(1, cols):
            slot = gwr.at[g, d]
            remote(slot, slot, g_send.at[g, d], g_recv.at[g, d], column(d), t).wait_recv()
            total = total + gwr[g, d].astype(f32)
        lanes = slice(g * HEAD_SIZE, (g + 1) * HEAD_SIZE)
        gwk_out[:, lanes] = total[:, :HEAD_SIZE]
        gwv_out[:, lanes] = total[:, HEAD_SIZE:]
    for copy in sends:
        copy.wait_send()
    for g in range(kv_heads):
        for d in range(1, SPAN):

            @pl.when(j + d < SPAN)
            def _():
                kv_copy(g, d).wait_send()

            @pl.when(j >= d)
            def _():
                grad_copy(g, d).wait_send()


def fused_device(hidden_states, query, attention_output_gradient, key_weight, value_weight, doc_start):
    tokens, width = hidden_states.shape
    depth, half = key_weight.shape
    count_cp = lax.axis_size("cp")
    cols = count_cp // PLANE
    per_tp = cols // 2
    kv_heads = half // HEAD_SIZE
    q_per_kv = query.shape[1] // half
    stack = q_per_kv * tokens
    pair = 2 * HEAD_SIZE
    bf16, f32 = jnp.bfloat16, jnp.float32
    starts = jnp.broadcast_to(doc_start[None, :], (8, tokens))[:1]
    dma = pltpu.SemaphoreType.DMA
    vmem = pltpu.VMEM
    spec = pl.BlockSpec(memory_space=pltpu.VMEM)
    return pl.pallas_call(
        functools.partial(exchange_kernel, count_cp, kv_heads, q_per_kv),
        out_shape=(
            jax.ShapeDtypeStruct(query.shape, bf16),
            jax.ShapeDtypeStruct((tokens, 2 * width), bf16),
            jax.ShapeDtypeStruct((depth, half), f32),
            jax.ShapeDtypeStruct((depth, half), f32),
        ),
        in_specs=[spec] * 6,
        out_specs=(spec,) * 4,
        scratch_shapes=[
            vmem((cols, PLANE, tokens, depth), bf16),
            vmem((kv_heads, cols, depth, pair), bf16),
            vmem((kv_heads, per_tp, depth, pair), bf16),
            vmem((kv_heads, PLANE, tokens, pair), f32),
            vmem((kv_heads, PLANE, tokens, pair), f32),
            vmem((kv_heads, SPAN, tokens, pair), bf16),
            vmem((kv_heads, stack, HEAD_SIZE), bf16),
            vmem((kv_heads, stack, HEAD_SIZE), bf16),
            vmem((SPAN, tokens, stack), f32),
            vmem((SPAN, tokens, stack), f32),
            vmem((HEAD_SIZE, stack), f32),
            vmem((kv_heads, SPAN, tokens, pair), f32),
            vmem((kv_heads, SPAN, tokens, pair), bf16),
            vmem((kv_heads, SPAN, tokens, pair), bf16),
            vmem((2, kv_heads, PLANE, tokens, pair), bf16),
            vmem((kv_heads, depth, pair), f32),
            vmem((kv_heads, cols, depth, pair), bf16),
            vmem((kv_heads, cols, depth, pair), bf16),
            vmem((PLANE, per_tp, tokens, depth), bf16),
            vmem((PLANE, 2, per_tp, tokens, depth), bf16),
            dma((2, PLANE, per_tp)),
            dma((2, PLANE, per_tp)),
            dma((kv_heads, cols)),
            dma((kv_heads, cols)),
            dma((kv_heads, per_tp)),
            dma((kv_heads, per_tp)),
            dma((kv_heads, PLANE)),
            dma((kv_heads, PLANE)),
            dma((kv_heads, SPAN)),
            dma((kv_heads, SPAN)),
            dma((kv_heads, SPAN)),
            dma((kv_heads, SPAN)),
            dma((kv_heads, 2, PLANE)),
            dma((2, kv_heads, PLANE)),
            dma((kv_heads, cols)),
            dma((kv_heads, cols)),
            dma((2, PLANE)),
            dma((PLANE, 2)),
        ],
        compiler_params=pltpu.CompilerParams(
            collective_id=0, has_side_effects=True, vmem_limit_bytes=56 * 1024 * 1024
        ),
    )(hidden_states, query, attention_output_gradient, key_weight, value_weight, starts)


def solution(mesh):
    def run(*arrays):
        fits = fused_fits(mesh, arrays[0].shape[1], arrays[0].shape[0])
        return jax.shard_map(
            fused_device if fits else per_device,
            mesh=mesh,
            in_specs=(P("cp", "tp"),) * 5 + (P("cp"),),
            out_specs=(P("cp", "tp"), P("cp", None), P("cp", "tp"), P("cp", "tp")),
            check_vma=False,
        )(*arrays)

    return run
```

```python
import functools

import jax
import jax.numpy as jnp
from jax import lax
from jax.experimental import pallas as pl
from jax.experimental.pallas import tpu as pltpu
from jax.sharding import PartitionSpec as P

HEAD_SIZE = 128
SPAN = 8


NEG_FILL = -1e30


def passed_along(value, axis, steps):
    count = lax.axis_size(axis)
    leading, last = (max(0, -steps), min(count, count - steps))
    return lax.ppermute(value, axis, [(source, source + steps) for source in range(leading, last)])


def from_behind(block, axis, distance):
    devices = range(lax.axis_size(axis))
    route = [((i - distance) % len(devices), i) for i in devices]
    return lax.ppermute(block, axis, route)


def split_pair(kv_block, heads_kv):
    row_count = kv_block.shape[0]
    kv_width = kv_block.shape[1] // 2
    key_part = kv_block[:, :kv_width].reshape(row_count, heads_kv, HEAD_SIZE)
    value_part = kv_block[:, kv_width:].reshape(row_count, heads_kv, HEAD_SIZE)
    return (key_part, value_part)


def forward_tile(running, query_heads, kv_block, visible_now, inv_sqrt):
    row_max, row_total, weighted = running
    key_part, value_part = split_pair(kv_block, query_heads.shape[1])
    scores = (
        jnp.einsum("qgrd,kgd->grqk", query_heads, key_part, preferred_element_type=jnp.float32)
        * inv_sqrt
    )
    scores = jnp.where(visible_now, scores, NEG_FILL)
    new_max = jnp.maximum(row_max, jnp.max(scores, axis=-1))
    probs_now = jnp.where(visible_now, jnp.exp(scores - new_max[..., None]), 0.0)
    fading = jnp.exp(row_max - new_max)
    new_total = row_total * fading + jnp.sum(probs_now, axis=-1)
    added = jnp.einsum(
        "grqk,kgd->grqd", probs_now, value_part.astype(jnp.float32), precision=lax.Precision.HIGHEST
    )
    return (new_max, new_total, weighted * fading[..., None] + added)


def backward_tile(query_heads, grad_heads, log_total, delta_rows, kv_block, visible_now, inv_sqrt):
    row_count = query_heads.shape[0]
    key_part, value_part = split_pair(kv_block, query_heads.shape[1])
    scores = (
        jnp.einsum("qgrd,kgd->grqk", query_heads, key_part, preferred_element_type=jnp.float32)
        * inv_sqrt
    )
    scores = jnp.where(visible_now, scores, NEG_FILL)
    probs_now = jnp.where(visible_now, jnp.exp(scores - log_total[..., None]), 0.0)
    value_gradient_total = jnp.einsum(
        "grqk,qgrd->kgd",
        probs_now.astype(jnp.bfloat16),
        grad_heads,
        preferred_element_type=jnp.float32,
    )
    prob_grad = jnp.einsum(
        "qgrd,kgd->grqk", grad_heads, value_part, preferred_element_type=jnp.float32
    )
    score_grad = (probs_now * (prob_grad - delta_rows[..., None])).astype(jnp.bfloat16)
    query_grad = (
        jnp.einsum("grqk,kgd->qgrd", score_grad, key_part, preferred_element_type=jnp.float32)
        * inv_sqrt
    )
    key_gradient_total = (
        jnp.einsum("grqk,qgrd->kgd", score_grad, query_heads, preferred_element_type=jnp.float32)
        * inv_sqrt
    )
    paired_gradient = jnp.concatenate(
        [key_gradient_total.reshape(row_count, -1), value_gradient_total.reshape(row_count, -1)],
        axis=1,
    )
    return (query_grad.reshape(row_count, -1), paired_gradient)


def per_device(
    hidden_states, query, attention_output_gradient, key_weight, value_projection_weight, doc_start
):
    row_count = query.shape[0]
    node_count = lax.axis_size("cp")
    my_index = lax.axis_index("cp")
    chain_len = min(SPAN, node_count // 2)
    kv_width = key_weight.shape[1]
    heads_kv = kv_width // HEAD_SIZE
    query_per_key_heads = query.shape[1] // kv_width
    inv_sqrt = HEAD_SIZE ** (-0.5)
    features = lax.all_gather(hidden_states, "tp", axis=1, tiled=True)
    key_full, value_full = (
        lax.all_gather(key_weight, "cp", axis=0, tiled=True),
        lax.all_gather(value_projection_weight, "cp", axis=0, tiled=True),
    )
    key_rows = jnp.dot(features, key_full, preferred_element_type=jnp.float32).astype(jnp.bfloat16)
    value_rows = jnp.dot(features, value_full, preferred_element_type=jnp.float32).astype(
        jnp.bfloat16
    )
    local_block = jnp.concatenate([key_rows, value_rows], axis=1)
    query_heads = query.reshape(row_count, heads_kv, query_per_key_heads, HEAD_SIZE)
    grad_heads = attention_output_gradient.reshape(
        row_count, heads_kv, query_per_key_heads, HEAD_SIZE
    )
    offsets = jnp.arange(row_count, dtype=jnp.int32)
    query_pos = my_index * row_count + offsets

    def visible(turn_index):
        source = my_index - turn_index
        key_pos = source * row_count + offsets
        return (
            (key_pos[None, :] >= doc_start[:, None])
            & (key_pos[None, :] <= query_pos[:, None])
            & (source >= 0)
        )

    start_stats = (
        jnp.full((heads_kv, query_per_key_heads, row_count), NEG_FILL, jnp.float32),
        jnp.zeros((heads_kv, query_per_key_heads, row_count), jnp.float32),
        jnp.zeros((heads_kv, query_per_key_heads, row_count, HEAD_SIZE), jnp.float32),
    )
    running = forward_tile(start_stats, query_heads, local_block, visible(0), inv_sqrt)
    stored = jnp.zeros((1,), jnp.bfloat16)

    def forward_turn(turn_index, carried):
        kv_block, stats_now, stored_now = carried
        kv_block = passed_along(kv_block, "cp", 1)
        visible_now = visible(turn_index)
        stats_now = lax.cond(
            jnp.any(visible_now),
            lambda: forward_tile(stats_now, query_heads, kv_block, visible_now, inv_sqrt),
            lambda: stats_now,
        )
        return (kv_block, stats_now, stored_now)

    unused_block, running, stored = lax.fori_loop(
        1, chain_len, forward_turn, (local_block, running, stored)
    )
    row_max, row_total, weighted = running
    log_total = row_max + jnp.log(row_total)
    attended = weighted / row_total[..., None]
    delta_rows = jnp.einsum(
        "qgrd,grqd->grq", grad_heads.astype(jnp.float32), attended, precision=lax.Precision.HIGHEST
    )
    query_sum, kv_sums = backward_tile(
        query_heads, grad_heads, log_total, delta_rows, local_block, visible(0), inv_sqrt
    )

    def backward_turn(turn_index, carried):
        kv_block, sums_now, query_now = carried
        sums_now = from_behind(sums_now, "cp", 1)
        kv_block = passed_along(kv_block, "cp", 1)
        visible_now = visible(turn_index)
        query_part, pair_part = lax.cond(
            jnp.any(visible_now),
            lambda: backward_tile(
                query_heads, grad_heads, log_total, delta_rows, kv_block, visible_now, inv_sqrt
            ),
            lambda: (jnp.zeros_like(query_now), jnp.zeros_like(sums_now)),
        )
        return (kv_block, sums_now + pair_part, query_now + query_part)

    unused_last, kv_sums, query_sum = lax.fori_loop(
        1, chain_len, backward_turn, (local_block, kv_sums, query_sum)
    )
    returned = from_behind(kv_sums.astype(jnp.bfloat16), "cp", 1 - chain_len).astype(kv_sums.dtype)
    gradients_lowered = returned.astype(jnp.bfloat16)
    weight_sums = lax.psum_scatter(
        lax.dot_general(
            features,
            gradients_lowered,
            (((0,), (0,)), ((), ())),
            preferred_element_type=jnp.float32,
        ),
        "cp",
        scatter_dimension=0,
        tiled=True,
    )
    projection = jnp.concatenate([key_full, value_full], axis=1)
    input_part = lax.dot_general(
        gradients_lowered, projection, (((1,), (1,)), ((), ())), preferred_element_type=jnp.float32
    )
    grad_hidden = lax.psum(input_part, "tp").astype(jnp.bfloat16)
    return (
        query_sum.astype(jnp.bfloat16),
        grad_hidden,
        weight_sums[:, :kv_width],
        weight_sums[:, kv_width:],
    )


PLANE = 4


def fused_fits(mesh, model_width, tokens):
    cp, tp = mesh.shape["cp"], mesh.shape["tp"]
    if cp % SPAN or cp % (PLANE * tp) or SPAN % PLANE or tp != 2:
        return False
    return model_width % (cp * HEAD_SIZE) == 0 and tokens // cp == HEAD_SIZE


def exchange_kernel(
    count_cp,
    kv_heads,
    q_per_kv,
    hid,
    qry,
    gout,
    wk,
    wv,
    starts,
    dq_out,
    gh_out,
    gwk_out,
    gwv_out,
    xp,
    wz,
    wo,
    part,
    summed,
    kvg,
    qs,
    gs,
    s_scr,
    dp_scr,
    dqt,
    dpart,
    dsend,
    drecv,
    dkvp,
    gwown,
    gws,
    gwr,
    ghs,
    gho,
    x_send,
    x_recv,
    w_send,
    w_recv,
    o_send,
    o_recv,
    r_send,
    r_recv,
    k_send,
    k_recv,
    d_send,
    d_recv,
    p_send,
    p_recv,
    g_send,
    g_recv,
    h_send,
    h_recv,
):
    tokens = hid.shape[0]
    depth = wk.shape[0]
    pair = 2 * HEAD_SIZE
    cols = count_cp // PLANE
    per_tp = cols // 2
    stack = q_per_kv * tokens
    inv_sqrt = HEAD_SIZE ** (-0.5)
    f32 = jnp.float32
    bf16 = jnp.bfloat16
    c = lax.axis_index("cp")
    t = lax.axis_index("tp")
    ot = 1 - t
    z = c // PLANE
    p = c % PLANE
    j = c % SPAN
    base = c - j

    def remote(src, dst, ss, rs, cp, tp):
        return pltpu.make_async_remote_copy(
            src_ref=src,
            dst_ref=dst,
            send_sem=ss,
            recv_sem=rs,
            device_id=(cp, tp),
            device_id_type=pl.DeviceIdType.MESH,
        )

    def at_plane(pp):
        return z * PLANE + pp

    barrier = pltpu.get_barrier_semaphore()
    greeted = 0

    def greet(cp, tp):
        pl.semaphore_signal(
            barrier, inc=1, device_id=(cp, tp), device_id_type=pl.DeviceIdType.MESH
        )

    for d in range(1, SPAN):
        greet(base + (j + d) % SPAN, t)
        greeted += 1
    for d in range(PLANE):
        greet(at_plane((p + d) % PLANE), ot)
        greeted += 1
    planes = SPAN // PLANE
    for d in range(cols - planes):
        greet((((z // planes) * planes + planes + d) % cols) * PLANE + p, t)
        greeted += 1
    for g in range(kv_heads):
        lanes = slice(g * HEAD_SIZE, (g + 1) * HEAD_SIZE)
        wz[g, z, :, :HEAD_SIZE] = wk[:, lanes]
        wz[g, z, :, HEAD_SIZE:] = wv[:, lanes]
    pl.semaphore_wait(barrier, greeted)

    sends = []

    def column(d):
        return ((z + d) % cols) * PLANE + p

    def plane_peers():
        return [(tt, d) for tt in range(2) for d in range(PLANE) if tt or d]

    def send_weights(g):
        for d in range(1, cols):
            slot = wz.at[g, z]
            copy = remote(slot, slot, w_send.at[g, d], w_recv.at[g, z], column(d), t)
            copy.start()
            sends.append(copy)

    send_weights(0)
    for tt, d in plane_peers():
        pp = (p + d) % PLANE
        for k in range(per_tp):
            lane = pl.multiple_of((k * PLANE + pp) * depth, HEAD_SIZE)
            copy = remote(
                hid.at[:, pl.ds(lane, depth)],
                xp.at[t * per_tp + k, p],
                x_send.at[tt, d, k],
                x_recv.at[t, p, k],
                at_plane(pp),
                (t + tt) % 2,
            )
            copy.start()
            sends.append(copy)
    for k in range(per_tp):
        lane = pl.multiple_of((k * PLANE + p) * depth, HEAD_SIZE)
        xp[t * per_tp + k, p] = hid[:, pl.ds(lane, depth)]
    for h in range(kv_heads * q_per_kv):
        g, r = h // q_per_kv, h % q_per_kv
        lanes = slice(h * HEAD_SIZE, (h + 1) * HEAD_SIZE)
        qs[g, r * tokens : (r + 1) * tokens] = qry[:, lanes]
        gs[g, r * tokens : (r + 1) * tokens] = gout[:, lanes]

    for tt, d in plane_peers():
        src_t, src_p = (t + tt) % 2, (p + d) % PLANE
        for k in range(per_tp):
            slot = xp.at[src_t * per_tp + k, src_p]
            remote(
                slot, slot, x_send.at[tt, d, k], x_recv.at[src_t, src_p, k], at_plane(src_p), src_t
            ).wait_recv()

    def project(g):
        for d in range(1, cols):
            zz = (z + d) % cols
            slot = wz.at[g, zz]
            remote(slot, slot, w_send.at[g, d], w_recv.at[g, zz], column(d), t).wait_recv()
        if g < kv_heads - 1:
            send_weights(g + 1)
        for d in range(cols):
            zz = (z + d) % cols
            lhs = xp[zz].reshape(PLANE * tokens, depth)
            add = jnp.dot(lhs, wz[g, zz], preferred_element_type=f32)
            add = add.reshape(PLANE, tokens, pair)
            if d:
                part[g] += add
            else:
                part[g] = add
        for d in range(1, PLANE):
            pp = (p + d) % PLANE
            copy = remote(
                part.at[g, pp], summed.at[g, p], r_send.at[g, d], r_recv.at[g, p], at_plane(pp), t
            )
            copy.start()
            sends.append(copy)
        for k in range(per_tp):
            copy = remote(
                wz.at[g, ot * per_tp + k], wo.at[g, k], o_send.at[g, k], o_recv.at[g, k], c, ot
            )
            copy.start()
            sends.append(copy)

    def kv_copy(g, d):
        slot = kvg.at[g, j]
        return remote(slot, slot, k_send.at[g, d], k_recv.at[g, j], c + d, t)

    def finish_keys(g):
        total = part[g, p]
        for d in range(1, PLANE):
            pp = (p + d) % PLANE
            slot = summed.at[g, pp]
            remote(slot, slot, r_send.at[g, d], r_recv.at[g, pp], at_plane(pp), t).wait_recv()
            total = total + summed[g, pp]
        kvg[g, j] = total.astype(bf16)
        for d in reversed(range(1, SPAN)):

            @pl.when(j + d < SPAN)
            def _():
                kv_copy(g, d).start()

    row = lax.broadcasted_iota(jnp.int32, (tokens, tokens), 0)
    lane_index = lax.broadcasted_iota(jnp.int32, (tokens, tokens), 1)
    start_row = starts[...]

    def fold(value, op):
        return op(value.reshape(tokens // 8, 8, stack), axis=0)

    nt = (((1,), (1,)), ((), ()))
    tn = (((0,), (0,)), ((), ()))
    kcol = slice(0, HEAD_SIZE)
    vcol = slice(HEAD_SIZE, 2 * HEAD_SIZE)

    def grad_copy(g, d):
        return remote(
            dsend.at[g, d], drecv.at[g, d], d_send.at[g, d], d_recv.at[g, d], c - d, t
        )

    def attend(g, after_first, after_second):
        def first_pass(d, top):
            i = j - d

            @pl.when(d > 0)
            def _():
                slot = kvg.at[g, i]
                remote(slot, slot, k_send.at[g, 1], k_recv.at[g, i], c - d, t).wait_recv()

            key_pos = (base + i) * tokens + row
            seen = (key_pos >= start_row) & (key_pos <= c * tokens + lane_index)
            bias = jnp.where(seen, 0.0, NEG_FILL)
            bias = jnp.concatenate([bias] * q_per_kv, axis=1)
            s = lax.dot_general(kvg[g, i, :, kcol], qs[g], nt, preferred_element_type=f32)
            s = s * inv_sqrt + bias
            s_scr[i] = s
            dp_scr[i] = lax.dot_general(
                kvg[g, i, :, vcol], gs[g], nt, preferred_element_type=f32
            )
            return jnp.maximum(top, fold(s, jnp.max))

        top = lax.fori_loop(0, j + 1, first_pass, jnp.full((8, stack), NEG_FILL, f32))
        top = jnp.max(top, axis=0, keepdims=True)
        after_first()

        def second_pass(i, carried):
            count, dot = carried
            e = jnp.exp(s_scr[i] - top)
            s_scr[i] = e
            return count + fold(e, jnp.sum), dot + fold(e * dp_scr[i], jnp.sum)

        zero = jnp.zeros((8, stack), f32)
        count, dot = lax.fori_loop(0, j + 1, second_pass, (zero, zero))
        inv_count = 1.0 / jnp.sum(count, axis=0, keepdims=True)
        delta = jnp.sum(dot, axis=0, keepdims=True) * inv_count
        after_second()
        dqt[...] = jnp.zeros_like(dqt)

        def third_pass(i, carried):
            probs = s_scr[i] * inv_count
            ds = (probs * (dp_scr[i] - delta)).astype(bf16)
            dpart[g, i, :, vcol] = jnp.dot(probs.astype(bf16), gs[g], preferred_element_type=f32)
            dpart[g, i, :, kcol] = jnp.dot(ds, qs[g], preferred_element_type=f32) * inv_sqrt
            dqt[...] += lax.dot_general(kvg[g, i, :, kcol], ds, tn, preferred_element_type=f32)
            return carried

        lax.fori_loop(0, j + 1, third_pass, 0)
        for d in range(1, SPAN):

            @pl.when(j >= d)
            def _():
                dsend[g, d] = dpart[g, j - d].astype(bf16)
                grad_copy(g, d).start()

        for r in range(q_per_kv):
            h = g * q_per_kv + r
            tile = dqt[:, r * tokens : (r + 1) * tokens]
            dq_out[:, h * HEAD_SIZE : (h + 1) * HEAD_SIZE] = (tile.T * inv_sqrt).astype(bf16)

    def collect(g):
        dpart[g, 0] = dpart[g, j]
        for d in range(1, SPAN):

            @pl.when(j + d < SPAN)
            def _():
                slot = drecv.at[g, d]
                remote(slot, slot, d_send.at[g, d], d_recv.at[g, d], c + d, t).wait_recv()
                dpart[g, 0] += drecv[g, d].astype(f32)

        dkvp[t, g, p] = dpart[g, 0].astype(bf16)
        for tt, d in plane_peers():
            slot = dkvp.at[t, g, p]
            copy = remote(
                slot,
                slot,
                p_send.at[g, tt, d],
                p_recv.at[t, g, p],
                at_plane((p + d) % PLANE),
                (t + tt) % 2,
            )
            copy.start()
            sends.append(copy)

    def wait_plane(g, tt):
        for d in range(1 - tt, PLANE):
            src_t, src_p = (t + tt) % 2, (p + d) % PLANE
            slot = dkvp.at[src_t, g, src_p]
            remote(
                slot, slot, p_send.at[g, tt, d], p_recv.at[src_t, g, src_p], at_plane(src_p), src_t
            ).wait_recv()

    def plane_grads(tt, g):
        return dkvp[tt, g].reshape(PLANE * tokens, pair)

    def weight_part(g, zz):
        lhs = xp[zz].reshape(PLANE * tokens, depth)
        return lax.dot_general(lhs, plane_grads(t, g), tn, preferred_element_type=f32)

    def send_weight_grads(g):
        for d in range(1, cols):
            gws[g, d] = weight_part(g, (z + d) % cols).astype(bf16)
            copy = remote(
                gws.at[g, d], gwr.at[g, d], g_send.at[g, d], g_recv.at[g, d], column(d), t
            )
            copy.start()
            sends.append(copy)

    def nothing():
        pass

    last = kv_heads - 1
    project(0)
    finish_keys(0)
    for g in range(kv_heads):
        if g < last:
            project(g + 1)
        attend(
            g,
            nothing,
            functools.partial(finish_keys, g + 1) if g < last else nothing,
        )
        if g:
            collect(g - 1)
            wait_plane(g - 1, 0)
            send_weight_grads(g - 1)
    collect(last)
    wait_plane(last, 0)
    send_weight_grads(last)
    for g in range(kv_heads):
        wait_plane(g, 1)
        for k in range(per_tp):
            slot = wo.at[g, k]
            remote(slot, slot, o_send.at[g, k], o_recv.at[g, k], c, ot).wait_recv()
    for k in range(per_tp):
        value = jnp.zeros((PLANE * tokens, depth), f32)
        for g in range(kv_heads):
            value += lax.dot_general(
                plane_grads(t, g), wz[g, t * per_tp + k], nt, preferred_element_type=f32
            )
            value += lax.dot_general(
                plane_grads(ot, g), wo[g, k], nt, preferred_element_type=f32
            )
        ghs[:, k] = value.astype(bf16).reshape(PLANE, tokens, depth)
    for tt, d in plane_peers():
        pp = (p + d) % PLANE
        copy = remote(
            ghs.at[pp], gho.at[p, t], h_send.at[tt, d], h_recv.at[p, t], at_plane(pp), (t + tt) % 2
        )
        copy.start()
        sends.append(copy)
    gho[p, t] = ghs[p]
    for g in range(kv_heads):
        gwown[g] = weight_part(g, z)
    for tt, d in plane_peers():
        src_t, src_p = (t + tt) % 2, (p + d) % PLANE
        slot = gho.at[src_p, src_t]
        remote(
            slot, slot, h_send.at[tt, d], h_recv.at[src_p, src_t], at_plane(src_p), src_t
        ).wait_recv()
    for zz in range(cols):
        for pp in range(PLANE):
            block = (zz * PLANE + pp) * depth
            gh_out[:, block : block + depth] = gho[pp, zz // per_tp, zz % per_tp]
    for g in range(kv_heads):
        total = gwown[g]
        for d in range(1, cols):
            slot = gwr.at[g, d]
            remote(slot, slot, g_send.at[g, d], g_recv.at[g, d], column(d), t).wait_recv()
            total = total + gwr[g, d].astype(f32)
        lanes = slice(g * HEAD_SIZE, (g + 1) * HEAD_SIZE)
        gwk_out[:, lanes] = total[:, :HEAD_SIZE]
        gwv_out[:, lanes] = total[:, HEAD_SIZE:]
    for copy in sends:
        copy.wait_send()
    for g in range(kv_heads):
        for d in range(1, SPAN):

            @pl.when(j + d < SPAN)
            def _():
                kv_copy(g, d).wait_send()

            @pl.when(j >= d)
            def _():
                grad_copy(g, d).wait_send()


def fused_device(hidden_states, query, attention_output_gradient, key_weight, value_weight, doc_start):
    tokens, width = hidden_states.shape
    depth, half = key_weight.shape
    count_cp = lax.axis_size("cp")
    cols = count_cp // PLANE
    per_tp = cols // 2
    kv_heads = half // HEAD_SIZE
    q_per_kv = query.shape[1] // half
    stack = q_per_kv * tokens
    pair = 2 * HEAD_SIZE
    bf16, f32 = jnp.bfloat16, jnp.float32
    starts = jnp.broadcast_to(doc_start[None, :], (8, tokens))[:1]
    dma = pltpu.SemaphoreType.DMA
    vmem = pltpu.VMEM
    spec = pl.BlockSpec(memory_space=pltpu.VMEM)
    return pl.pallas_call(
        functools.partial(exchange_kernel, count_cp, kv_heads, q_per_kv),
        out_shape=(
            jax.ShapeDtypeStruct(query.shape, bf16),
            jax.ShapeDtypeStruct((tokens, 2 * width), bf16),
            jax.ShapeDtypeStruct((depth, half), f32),
            jax.ShapeDtypeStruct((depth, half), f32),
        ),
        in_specs=[spec] * 6,
        out_specs=(spec,) * 4,
        scratch_shapes=[
            vmem((cols, PLANE, tokens, depth), bf16),
            vmem((kv_heads, cols, depth, pair), bf16),
            vmem((kv_heads, per_tp, depth, pair), bf16),
            vmem((kv_heads, PLANE, tokens, pair), f32),
            vmem((kv_heads, PLANE, tokens, pair), f32),
            vmem((kv_heads, SPAN, tokens, pair), bf16),
            vmem((kv_heads, stack, HEAD_SIZE), bf16),
            vmem((kv_heads, stack, HEAD_SIZE), bf16),
            vmem((SPAN, tokens, stack), f32),
            vmem((SPAN, tokens, stack), f32),
            vmem((HEAD_SIZE, stack), f32),
            vmem((kv_heads, SPAN, tokens, pair), f32),
            vmem((kv_heads, SPAN, tokens, pair), bf16),
            vmem((kv_heads, SPAN, tokens, pair), bf16),
            vmem((2, kv_heads, PLANE, tokens, pair), bf16),
            vmem((kv_heads, depth, pair), f32),
            vmem((kv_heads, cols, depth, pair), bf16),
            vmem((kv_heads, cols, depth, pair), bf16),
            vmem((PLANE, per_tp, tokens, depth), bf16),
            vmem((PLANE, 2, per_tp, tokens, depth), bf16),
            dma((2, PLANE, per_tp)),
            dma((2, PLANE, per_tp)),
            dma((kv_heads, cols)),
            dma((kv_heads, cols)),
            dma((kv_heads, per_tp)),
            dma((kv_heads, per_tp)),
            dma((kv_heads, PLANE)),
            dma((kv_heads, PLANE)),
            dma((kv_heads, SPAN)),
            dma((kv_heads, SPAN)),
            dma((kv_heads, SPAN)),
            dma((kv_heads, SPAN)),
            dma((kv_heads, 2, PLANE)),
            dma((2, kv_heads, PLANE)),
            dma((kv_heads, cols)),
            dma((kv_heads, cols)),
            dma((2, PLANE)),
            dma((PLANE, 2)),
        ],
        compiler_params=pltpu.CompilerParams(
            collective_id=0, has_side_effects=True, vmem_limit_bytes=56 * 1024 * 1024
        ),
    )(hidden_states, query, attention_output_gradient, key_weight, value_weight, starts)


def solution(mesh):
    def run(*arrays):
        fits = fused_fits(mesh, arrays[0].shape[1], arrays[0].shape[0])
        return jax.shard_map(
            fused_device if fits else per_device,
            mesh=mesh,
            in_specs=(P("cp", "tp"),) * 5 + (P("cp"),),
            out_specs=(P("cp", "tp"), P("cp", None), P("cp", "tp"), P("cp", "tp")),
            check_vma=False,
        )(*arrays)

    return run
```
